32 devices in a mesh: rep: 2 (over x), gx: 16 (over z, y, core).
Axes of the slice: x: 2, y: 2, z: 4, core: 2. Of those that a mesh axis runs over, the one named last changes fastest.
Arguments:
- inputs: bfloat16 [2, 64, 18432], P(None, 'rep', 'gx'), parts along dimension 1, may hold values from -450 to 450, as said below
- gain: bfloat16 [18432], P('gx'), may hold values from 0.5 to 1.5
- w_query: bfloat16 [18432, 12288], P(None, 'gx'), may hold values from -0.046875 to 0.046875
- w_keyval: bfloat16 [18432, 512], P('gx'), may hold values from -0.046875 to 0.046875
- w_out: bfloat16 [12288, 18432], P(None, 'gx'), may hold values from -0.0546875 to 0.0546875
- key_cache: bfloat16 [64, 2048, 256], P(('rep', 'gx')), parts along dimension 0, may hold values from -240 to 240
- value_cache: bfloat16 [64, 2048, 256], P(('rep', 'gx')), parts along dimension 0, may hold values from -6 to 6
- lengths: int32 [64], P(('rep', 'gx')), parts along dimension 0, may hold values from 1 to 2048, 32768 in all
Outputs:
- branch: bfloat16 [2, 64, 18432], P(None, 'rep', 'gx'), parts along dimension 1
The draws below stay inside these ranges and needn't reach their ends.
There are 2 independent parts, one for each index of `rep`. The reference program is written for one: setup_inputs(seed, part) draws one part's arguments, and reference() takes and returns one part's arrays. A program takes and returns all parts, laid end to end along the dimension named above; an argument that names none is the same for every part. Nothing has to cross between parts.
Inputs may be any that keep to these rules, and one draw needn't show every extreme that they name: `inputs`: activations. The lengths of each part along rep sum to 32768; at least one row has exactly 2048.
All inputs are finite; a program needn't handle non-finite values. No bound on the sum of `lengths` on one device may be relied on, other than what follows from the above.
Results may differ from the reference program's by a relative error of at most 0.0065.
The reference program's roundings to bfloat16 on the way count: a program that leaves them out, or rounds other values in their place, can miss the bound.
Values may be sent and summed in bfloat16 or wider, within the bound.
A program may use at most 192 MiB of HBM per device.

```python
import math
import jax
import jax.numpy as jnp
import numpy as np
from jax import lax

D = 18432
H = 48
DH = 256
CACHE = 2048
STEPS = 2
ROWS = 32


def draw_inputs(key, part):
    key = jax.random.fold_in(key, 11)
    streams = jax.random.split(key, 3)
    shape = (STEPS, ROWS, D)
    base = jnp.clip(jax.random.normal(streams[0], shape, jnp.float32), -4.0, 4.0)
    row_scale = jnp.exp(jax.random.uniform(streams[1], (STEPS, ROWS, 1), jnp.float32, 0.0, math.log(10.0)))
    column_scale = jnp.exp(jax.random.uniform(streams[2], (D,), jnp.float32, 0.0, math.log(10.0)))
    return (base * row_scale * column_scale).astype(jnp.bfloat16)


def draw_key_cache(key, part):
    key = jax.random.fold_in(key, 23)
    streams = jax.random.split(key, 1)
    base = jnp.clip(jax.random.normal(streams[0], (ROWS, CACHE, DH), jnp.float32), -4.0, 4.0)
    return base.astype(jnp.bfloat16)


def steps_of(own_key, dims, shards, least, top_value):
    def one(dim, blocks):
        heights = jax.random.uniform(jax.random.fold_in(jax.random.fold_in(own_key, 6), dim), (blocks,), jnp.float32, least / len(shards), top_value / len(shards))
        return jnp.repeat(jnp.exp(heights), dims[dim] // blocks).reshape((-1,) + (1,) * (len(dims) - dim - 1))

    factor_of = one(*shards[0])
    for cut in shards[1:]:
        factor_of = factor_of * one(*cut)
    return factor_of


def profile(count, total, bound, lean):
    weights = [(1 << 20) // math.isqrt(grade ** lean) + 1 for grade in range(2, count + 1)]
    spare, counts = total - bound - (count - 1), [1] * (count - 1)
    while spare > 0:
        free = [i for i in range(count - 1) if counts[i] < bound]
        mass, remaining = sum([weights[i] for i in free]), spare
        for i in free:
            extra = min(bound - counts[i], max(1, remaining * weights[i] // mass), spare)
            counts[i] = counts[i] + extra
            spare = spare - extra
    return np.array([bound] + counts)


def ragged_sizes(rng, count, total, reach, slope):
    if count == 2:
        one = jax.random.randint(rng, (), max(1, total - reach), min(reach, total - 1) + 1)
        return jnp.stack([one, total - one])
    tallies = jnp.asarray(profile(count, total, reach, slope), jnp.int32)
    twos = (count - 1) // 2
    donor, sink = tallies[1:1 + 2 * twos:2], tallies[2:2 + 2 * twos:2]
    slack = jnp.minimum(donor - 1, reach - sink)
    moved = jax.random.randint(jax.random.fold_in(rng, 1), (twos,), 0, 1 << 20) % (slack + 1)
    tallies = tallies.at[1:1 + 2 * twos:2].set(donor - moved).at[2:2 + 2 * twos:2].set(sink + moved)
    return tallies[jax.random.permutation(jax.random.fold_in(rng, 2), count)]


def normal_values(key, dims, spread, limit, pieces=(), held_as=jnp.bfloat16):
    array = jax.random.normal(key, dims, jnp.float32) * spread
    if len(pieces) > 0:
        array = steps_of(key, dims, pieces, -0.22, 0.18) * array
    return jnp.clip(array, min=-limit, max=limit).astype(held_as)


def setup_inputs(seed: int = 0, part: int = 0) -> dict:
    key_of = jax.random.split(jax.random.key(seed), 9)
    own_keys = jax.random.split(jax.random.fold_in(key_of[8], part), 9)
    inputs = draw_inputs(jax.random.fold_in(jax.random.fold_in(key_of[8], part), 71), part)
    gain = jnp.clip(1.0 + 0.1 * jax.random.normal(key_of[1], (D,), jnp.float32), 0.5, 1.5).astype(jnp.bfloat16)
    w_query = normal_values(key_of[2], (D, H * DH), D ** -0.5, 0.046875, ((1, 16),))
    w_keyval = normal_values(key_of[3], (D, 2 * DH), D ** -0.5, 0.046875, ((0, 16),))
    w_out = normal_values(key_of[4], (H * DH, D), (H * DH) ** -0.5, 0.0546875, ((1, 16),))
    key_cache = draw_key_cache(jax.random.fold_in(jax.random.fold_in(key_of[8], part), 71), part)
    value_cache = normal_values(own_keys[6], (ROWS, CACHE, DH), 1.0, 6.0, ((0, 16),))
    lengths = ragged_sizes(own_keys[7], ROWS, ROWS * CACHE // 2, CACHE, 0).astype(jnp.int32)
    return dict(inputs=inputs, gain=gain, w_query=w_query, w_keyval=w_keyval, w_out=w_out, key_cache=key_cache, value_cache=value_cache, lengths=lengths)


EPS = 1e-05

def attend_row(packed):
    query_row, keys_row, values_row, fresh_keys, fresh_values, length = packed
    scale = DH ** (-0.5)
    cached = jnp.einsum('shd,cd->shc', query_row.astype(jnp.float32), keys_row.astype(jnp.float32)) * scale
    valid = lax.broadcasted_iota(jnp.int32, (1, 1, CACHE), 2) < length.astype(jnp.int32)
    cached = jnp.where(valid, cached, -jnp.inf)
    recent = jnp.einsum('shd,td->sht', query_row.astype(jnp.float32), fresh_keys.astype(jnp.float32)) * scale
    allowed = lax.broadcasted_iota(jnp.int32, (STEPS, 1, STEPS), 2) <= lax.broadcasted_iota(jnp.int32, (STEPS, 1, STEPS), 0)
    recent = jnp.where(allowed, recent, -jnp.inf)
    top = jnp.maximum(lax.optimization_barrier(jnp.max(cached, -1, keepdims=True)), lax.optimization_barrier(jnp.max(recent, -1, keepdims=True)))
    cached_exp = jnp.exp(cached - top)
    recent_exp = jnp.exp(recent - top)
    denom = lax.optimization_barrier(jnp.sum(cached_exp, -1, keepdims=True)) + lax.optimization_barrier(jnp.sum(recent_exp, -1, keepdims=True))
    cached_prob = (cached_exp / denom).astype(jnp.bfloat16)
    recent_prob = (recent_exp / denom).astype(jnp.bfloat16)
    result = jnp.einsum('shc,cd->shd', cached_prob.astype(jnp.float32), values_row.astype(jnp.float32))
    result = result + jnp.einsum('sht,td->shd', recent_prob.astype(jnp.float32), fresh_values.astype(jnp.float32))
    return result.astype(jnp.bfloat16).reshape(STEPS, H * DH)

def reference(inputs, gain, w_query, w_keyval, w_out, key_cache, value_cache, lengths):
    widened = inputs.astype(jnp.float32)
    row_mean = lax.optimization_barrier(jnp.mean(widened, -1, keepdims=True))
    row_square = lax.optimization_barrier(jnp.mean(widened * widened, -1, keepdims=True))
    normed = ((widened - row_mean) * lax.rsqrt(row_square - row_mean * row_mean + EPS) * gain.astype(jnp.float32)).astype(jnp.bfloat16)
    flat = normed.reshape(STEPS * ROWS, D)
    queries = jnp.dot(flat, w_query, preferred_element_type=jnp.float32).astype(jnp.bfloat16).reshape(STEPS, ROWS, H, DH)
    keyval = jnp.dot(flat, w_keyval, preferred_element_type=jnp.float32).astype(jnp.bfloat16).reshape(STEPS, ROWS, 2 * DH)
    new_keys = jnp.transpose(keyval[:, :, :DH], (1, 0, 2))
    new_values = jnp.transpose(keyval[:, :, DH:], (1, 0, 2))
    attended = lax.map(attend_row, (jnp.transpose(queries, (1, 0, 2, 3)), key_cache, value_cache, new_keys, new_values, lengths))
    attended = jnp.transpose(attended, (1, 0, 2)).reshape(STEPS * ROWS, H * DH)
    branch = jnp.dot(attended, w_out, preferred_element_type=jnp.float32).astype(jnp.bfloat16)
    return branch.reshape(STEPS, ROWS, D)
```

```python
import jax
import jax.numpy as jnp
import numpy as np
from jax import lax
from jax.experimental import pallas as pl
from jax.experimental.pallas import tpu as pltpu
from jax.sharding import PartitionSpec as P

D = 18432
H = 48
DH = 256


EPS = 1e-05


def collect_keyval(local_normed, w_keyval):
    summed = lax.psum_scatter(
        jnp.einsum("srk,kc->rsc", local_normed, w_keyval, preferred_element_type=jnp.float32),
        "gx",
        scatter_dimension=0,
        tiled=True,
    )
    return jnp.transpose(summed, (1, 0, 2)).astype(jnp.bfloat16)


def project(block, gain, w_query, w_keyval):
    widened = block.astype(jnp.float32)
    totals, squares = lax.psum((jnp.sum(widened, -1), jnp.sum(widened * widened, -1)), "gx")
    row_mean = (totals / D)[..., None]
    row_square = (squares / D)[..., None]
    normed = (
        (widened - row_mean)
        * lax.rsqrt(row_square - row_mean * row_mean + EPS)
        * gain.astype(jnp.float32)
    ).astype(jnp.bfloat16)
    portion = lax.all_gather(normed, "gx", axis=2, tiled=True)
    flat = portion.reshape(-1, portion.shape[2])
    query_part = jnp.dot(flat, w_query, preferred_element_type=jnp.float32).reshape(
        block.shape[0], block.shape[1], w_query.shape[1]
    )
    keyvals = collect_keyval(normed, w_keyval)
    return (query_part.astype(jnp.bfloat16), keyvals)


def attend(queries, key_cache, value_cache, lengths, fresh_keys, fresh_values):
    steps = queries.shape[0]
    rows_here = queries.shape[1]
    scale = DH ** (-0.5)
    grid = queries.reshape(steps, rows_here, H, DH)
    cached = (
        jnp.einsum("srhd,rcd->srhc", grid, key_cache, preferred_element_type=jnp.float32) * scale
    )
    valid = (
        lax.broadcasted_iota(jnp.int32, (1, rows_here, 1, key_cache.shape[1]), 3)
        < lengths[None, :, None, None]
    )
    cached = jnp.where(valid, cached, -jnp.inf)
    recent = (
        jnp.einsum("srhd,trd->srht", grid, fresh_keys, preferred_element_type=jnp.float32) * scale
    )
    allowed = lax.broadcasted_iota(jnp.int32, (steps, 1, 1, steps), 3) <= lax.broadcasted_iota(
        jnp.int32, (steps, 1, 1, steps), 0
    )
    recent = jnp.where(allowed, recent, -jnp.inf)
    top = jnp.maximum(jnp.max(cached, -1, keepdims=True), jnp.max(recent, -1, keepdims=True))
    cached_exp = jnp.exp(cached - top)
    recent_exp = jnp.exp(recent - top)
    denom = jnp.sum(cached_exp, -1, keepdims=True) + jnp.sum(recent_exp, -1, keepdims=True)
    cached_prob = (cached_exp / denom).astype(jnp.bfloat16)
    recent_prob = (recent_exp / denom).astype(jnp.bfloat16)
    result = jnp.einsum(
        "srhc,rcd->srhd", cached_prob, value_cache, preferred_element_type=jnp.float32
    )
    result = result + jnp.einsum(
        "srht,trd->srhd", recent_prob, fresh_values, preferred_element_type=jnp.float32
    )
    return result.astype(jnp.bfloat16).reshape(steps, rows_here, H * DH)


def finish(attended, w_out):
    portion = lax.all_gather(attended, "gx", axis=1, tiled=True)
    flat = portion.reshape(-1, portion.shape[2])
    product = jnp.dot(flat, w_out, preferred_element_type=jnp.float32)
    return product.reshape(portion.shape[0], portion.shape[1], w_out.shape[1]).astype(jnp.bfloat16)


def body(inputs, gain, w_query, w_keyval, w_out, key_cache, value_cache, lengths):
    queries, keyvals = project(inputs, gain, w_query, w_keyval)
    queries = lax.all_to_all(queries, "gx", split_axis=1, concat_axis=2, tiled=True)
    attended = attend(
        queries, key_cache, value_cache, lengths, keyvals[:, :, :DH], keyvals[:, :, DH:]
    )
    return finish(attended, w_out)


def solution(mesh):
    in_specs = (
        P(None, "rep", "gx"),
        P("gx"),
        P(None, "gx"),
        P("gx", None),
        P(None, "gx"),
        P(("rep", "gx"), None, None),
        P(("rep", "gx"), None, None),
        P(("rep", "gx")),
    )
    out_specs = P(None, "rep", "gx")
    return jax.shard_map(body, mesh=mesh, in_specs=in_specs, out_specs=out_specs, check_vma=False)
```

```python
import jax
import jax.numpy as jnp
import numpy as np
from jax import lax
from jax.experimental import pallas as pl
from jax.experimental.pallas import tpu as pltpu
from jax.sharding import PartitionSpec as P

D = 18432
H = 48
DH = 256
CACHE = 2048


EPS = 1e-05


def collect_keyval(local_normed, w_keyval):
    summed = lax.psum_scatter(
        jnp.einsum("srk,kc->rsc", local_normed, w_keyval, preferred_element_type=jnp.float32),
        "gx",
        scatter_dimension=0,
        tiled=True,
    )
    return jnp.transpose(summed, (1, 0, 2)).astype(jnp.bfloat16)


def project(block, gain, w_query, w_keyval):
    widened = block.astype(jnp.float32)
    totals, squares = lax.psum((jnp.sum(widened, -1), jnp.sum(widened * widened, -1)), "gx")
    row_mean = (totals / D)[..., None]
    row_square = (squares / D)[..., None]
    normed = (
        (widened - row_mean)
        * lax.rsqrt(row_square - row_mean * row_mean + EPS)
        * gain.astype(jnp.float32)
    ).astype(jnp.bfloat16)
    portion = lax.all_gather(normed, "gx", axis=2, tiled=True)
    flat = portion.reshape(-1, portion.shape[2])
    query_part = jnp.dot(flat, w_query, preferred_element_type=jnp.float32).reshape(
        block.shape[0], block.shape[1], w_query.shape[1]
    )
    keyvals = collect_keyval(normed, w_keyval)
    return (query_part.astype(jnp.bfloat16), keyvals)


def attend(queries, key_cache, value_cache, lengths, fresh_keys, fresh_values):
    steps = queries.shape[0]
    rows_here = queries.shape[1]
    scale = DH ** (-0.5)
    grid = queries.reshape(steps, rows_here, H, DH)
    cached = (
        jnp.einsum("srhd,rcd->srhc", grid, key_cache, preferred_element_type=jnp.float32) * scale
    )
    valid = (
        lax.broadcasted_iota(jnp.int32, (1, rows_here, 1, key_cache.shape[1]), 3)
        < lengths[None, :, None, None]
    )
    cached = jnp.where(valid, cached, -jnp.inf)
    recent = (
        jnp.einsum("srhd,trd->srht", grid, fresh_keys, preferred_element_type=jnp.float32) * scale
    )
    allowed = lax.broadcasted_iota(jnp.int32, (steps, 1, 1, steps), 3) <= lax.broadcasted_iota(
        jnp.int32, (steps, 1, 1, steps), 0
    )
    recent = jnp.where(allowed, recent, -jnp.inf)
    top = jnp.maximum(jnp.max(cached, -1, keepdims=True), jnp.max(recent, -1, keepdims=True))
    cached_exp = jnp.exp(cached - top)
    recent_exp = jnp.exp(recent - top)
    denom = jnp.sum(cached_exp, -1, keepdims=True) + jnp.sum(recent_exp, -1, keepdims=True)
    cached_prob = (cached_exp / denom).astype(jnp.bfloat16)
    recent_prob = (recent_exp / denom).astype(jnp.bfloat16)
    result = jnp.einsum(
        "srhc,rcd->srhd", cached_prob, value_cache, preferred_element_type=jnp.float32
    )
    result = result + jnp.einsum(
        "srht,trd->srhd", recent_prob, fresh_values, preferred_element_type=jnp.float32
    )
    return result.astype(jnp.bfloat16).reshape(steps, rows_here, H * DH)


def finish(attended, w_out):
    portion = lax.all_gather(attended, "gx", axis=1, tiled=True)
    flat = portion.reshape(-1, portion.shape[2])
    product = jnp.dot(flat, w_out, preferred_element_type=jnp.float32)
    return product.reshape(portion.shape[0], portion.shape[1], w_out.shape[1]).astype(jnp.bfloat16)


def body(inputs, gain, w_query, w_keyval, w_out, key_cache, value_cache, lengths):
    queries, keyvals = project(inputs, gain, w_query, w_keyval)
    queries = lax.all_to_all(queries, "gx", split_axis=1, concat_axis=2, tiled=True)
    attended = attend(
        queries, key_cache, value_cache, lengths, keyvals[:, :, :DH], keyvals[:, :, DH:]
    )
    return finish(attended, w_out)


GROUP = 16
WIDTH = 1152
PART_ROWS = 64
QCOLS = 768
MESH = pl.DeviceIdType.MESH


def one_hots():
    scatter_q = np.zeros((3, 256, 64), np.float32)
    scatter_kv = np.zeros((128, 64), np.float32)
    pack = np.zeros((192, 256), np.float32)
    unpack = np.zeros((256, 256), np.float32)
    for j in range(16):
        for r in range(2):
            for s in range(2):
                row = s * 32 + 2 * j + r
                scatter_kv[j * 8 + r * 2 + s, row] = 1
                scatter_kv[j * 8 + 4 + r * 2 + s, row] = 1
                for h in range(3):
                    scatter_q[h, j * 16 + r * 8 + s * 3 + h, row] = 1
                    pack[(j * 3 + h) * 4 + r * 2 + s, r * 128 + j * 8 + s * 3 + h] = 1
                for h in range(4):
                    unpack[h * 64 + row, j * 16 + h * 4 + r * 2 + s] = 1
    return tuple(jnp.asarray(a, jnp.bfloat16) for a in (scatter_q, scatter_kv, pack, unpack))


def dot(a, b):
    return jnp.dot(a, b, preferred_element_type=jnp.float32)


def dot_t(a, b):
    return lax.dot_general(a, b, (((1,), (1,)), ((), ())), preferred_element_type=jnp.float32)


def fused_kernel(
    x_hbm, g_ref, wq_hbm, wkv_hbm, wo_hbm, kc_hbm, vc_hbm, len_ref, sq_hbm, skv_hbm, pack_hbm, unpack_hbm,
    o_ref,
    xg, w, wkv, kc, vc, sq, skv, pack, unpack, st_out, st_in, kv_out, kv_in, q_out, q_in, ag, xn, acc, oacc,
    load_sem, wq_sem, wo_sem, x_send, x_recv, a_send, a_recv, st_send, st_recv, kv_send, kv_recv, q_send, q_recv,
):
    me = lax.axis_index("gx")
    z = lax.div(me, 4)
    y = lax.rem(lax.div(me, 2), 2)
    c = lax.rem(me, 2)

    def slot_of(zo, yo, co):
        return zo * 4 + yo * 2 + co

    def order(k):
        near = jnp.minimum(z, 3 - z)
        o = k if k >= 2 else jnp.where(near == 0, k, 1 - k)
        return jnp.where(z >= 2, 3 - o, o)

    own_load = pltpu.make_async_copy(x_hbm, xg.at[me], load_sem.at[0])
    own_load.start()
    wkv_load = pltpu.make_async_copy(wkv_hbm, wkv, load_sem.at[1])
    wkv_load.start()
    skv_load = pltpu.make_async_copy(skv_hbm, skv, load_sem.at[2])
    skv_load.start()

    def wq_load(chip):
        rows = pl.ds(pl.multiple_of(chip * (2 * WIDTH), 2 * WIDTH), 2 * WIDTH)
        return pltpu.make_async_copy(wq_hbm.at[rows], w.at[rows], wq_sem.at[chip])

    chips = [(0, 0), (0, 1), (1, 0), (1, 1), (2, 0), (2, 1), (3, 0), (3, 1)]

    def chip_of(k, flip):
        return order(k) * 2 + (1 - y if flip else y)

    for k, flip in chips:
        wq_load(chip_of(k, flip)).start()
    late_loads = [
        pltpu.make_async_copy(sq_hbm, sq, load_sem.at[3]),
        pltpu.make_async_copy(kc_hbm, kc, load_sem.at[4]),
        pltpu.make_async_copy(vc_hbm, vc, load_sem.at[5]),
        pltpu.make_async_copy(pack_hbm, pack, load_sem.at[6]),
        pltpu.make_async_copy(unpack_hbm, unpack, load_sem.at[7]),
    ]
    for load in late_loads:
        load.start()

    barrier = pltpu.get_barrier_semaphore()
    for step in range(1, GROUP):
        pl.semaphore_signal(
            barrier, inc=1, device_id={"gx": lax.rem(me + step, GROUP)}, device_id_type=MESH
        )
    pl.semaphore_wait(barrier, GROUP - 1)

    def remote(src, dst, send, recv, dev):
        return pltpu.make_async_remote_copy(
            src_ref=src, dst_ref=dst, send_sem=send, recv_sem=recv, device_id={"gx": dev}, device_id_type=MESH
        )

    class Gather:
        def __init__(self, buf, send, recv):
            self.buf, self.send, self.recv = buf, send, recv

        def copy(self, slot, k, kind, dev):
            return remote(
                self.buf.at[slot], self.buf.at[slot], self.send.at[k, kind], self.recv.at[slot], dev
            )

        def arrive(self, slot):
            self.copy(slot, 0, 0, lax.rem(me + 1, GROUP)).wait_recv()

        def line(self, k, act):
            zo = order(k)
            slot = slot_of(zo, y, c)

            @pl.when(jnp.logical_and(zo <= z, z < 3))
            def _():
                act(self.copy(slot, k, 0, slot_of(z + 1, y, c)))

            @pl.when(jnp.logical_and(zo >= z, z > 0))
            def _():
                act(self.copy(slot, k, 1, slot_of(z - 1, y, c)))

            act(self.copy(slot, k, 2, slot_of(z, 1 - y, c)))
            act(self.copy(slot, k, 3, slot_of(z, y, 1 - c)))

        def across(self, k, act):
            act(self.copy(slot_of(order(k), 1 - y, c), k, 4, slot_of(z, y, 1 - c)))

        def step_line(self, k):
            if k > 0:
                self.arrive(slot_of(order(k), y, c))
            self.line(k, lambda copy: copy.start())

        def step_across(self, k):
            self.arrive(slot_of(order(k), 1 - y, c))
            self.across(k, lambda copy: copy.start())

        def sibling(self, k, flip):
            self.arrive(slot_of(order(k), 1 - y if flip else y, 1 - c))

        def drain(self):
            for k in range(4):
                self.line(k, lambda copy: copy.wait_send())
                self.across(k, lambda copy: copy.wait_send())

    def spread(out, into, send, recv):
        def copy(step):
            target = lax.rem(me + step, GROUP)
            return remote(out.at[target], into.at[me], send.at[step], recv.at[me], target)

        for step in range(1, GROUP):
            copy(step).start()
        into[me] = out[me]
        return copy

    def collect(out, into, send, recv):
        for step in range(1, GROUP):
            source = lax.rem(me + step, GROUP)
            remote(out.at[source], into.at[source], send.at[step], recv.at[source], source).wait_recv()

    xs = Gather(xg, x_send, x_recv)
    own_load.wait()
    xs.step_line(0)

    x = xg[me]
    eye = lax.broadcasted_iota(jnp.int32, (PART_ROWS, PART_ROWS), 0) == lax.broadcasted_iota(
        jnp.int32, (PART_ROWS, PART_ROWS), 1
    )
    squares = jnp.sum(jnp.where(eye, dot_t(x, x), 0.0), axis=0, keepdims=True)
    sums = dot_t(jnp.ones((8, WIDTH), jnp.bfloat16), x)
    st_out[...] = jnp.zeros_like(st_out)
    st_out[0:9, :] = g_ref[...]
    st_out[9:10, 0:PART_ROWS] = sums[0:1]
    st_out[10:11, 0:PART_ROWS] = squares

    def st_copy(step):
        target = lax.rem(me + step, GROUP)
        return remote(st_out, st_in.at[me], st_send.at[step], st_recv.at[me], target)

    for step in range(1, GROUP):
        st_copy(step).start()
    st_in[me] = st_out[...]
    for step in range(1, GROUP):
        source = lax.rem(me + step, GROUP)
        remote(st_out, st_in.at[source], st_send.at[step], st_recv.at[source], source).wait_recv()

    total = st_in[0]
    for source in range(1, GROUP):
        total = total + st_in[source]

    def column(row):
        spread_row = jnp.broadcast_to(row, (PART_ROWS, PART_ROWS))
        return jnp.sum(jnp.where(eye, spread_row, 0.0), axis=1, keepdims=True)

    mean = column(total[9:10, 0:PART_ROWS]) / D
    square = column(total[10:11, 0:PART_ROWS]) / D
    factor = lax.rsqrt(square - mean * mean + EPS)

    def normed(slot):
        parts = st_in[slot]
        gain = jnp.concatenate([parts[i : i + 1, :] for i in range(9)], axis=1)
        return ((xg[slot].astype(jnp.float32) - mean) * factor * gain).astype(jnp.bfloat16)

    wkv_load.wait()
    skv_load.wait()
    ordered = dot(skv[...], normed(me)).astype(jnp.bfloat16)
    partial = dot(ordered, wkv[...])
    is_key = lax.rem(lax.broadcasted_iota(jnp.int32, (128, DH), 0), 8) < 4
    kv_out[...] = jnp.where(is_key, partial[:, :DH], partial[:, DH:]).reshape(GROUP, 8, DH)
    kv_copy = spread(kv_out, kv_in, kv_send, kv_recv)

    acc[...] = jnp.zeros_like(acc)

    def multiply(k, flip):
        chip = chip_of(k, flip)
        xs.sibling(k, flip)
        xn[:, 0:WIDTH] = normed(chip * 2)
        xn[:, WIDTH : 2 * WIDTH] = normed(chip * 2 + 1)
        wq_load(chip).wait()

        def tile(i, carry):
            rows = pl.ds(pl.multiple_of(chip * (2 * WIDTH) + i * 768, 768), 768)
            acc[...] += dot(xn[:, pl.ds(pl.multiple_of(i * 768, 768), 768)], w[rows, :])
            return carry

        lax.fori_loop(0, 3, tile, 0)

    xs.step_line(1)
    xs.step_across(0)
    multiply(0, 0)
    xs.step_line(2)
    xs.step_across(1)
    multiply(0, 1)
    multiply(1, 0)
    xs.step_line(3)
    xs.step_across(2)
    multiply(1, 1)
    multiply(2, 0)
    xs.step_across(3)
    multiply(2, 1)
    multiply(3, 0)
    multiply(3, 1)

    half = H * DH // 2
    rest = WIDTH - QCOLS
    wo_loads = [
        pltpu.make_async_copy(wo_hbm.at[:, pl.ds(0, QCOLS)], w.at[pl.ds(0, 2 * half)], wo_sem.at[0]),
        pltpu.make_async_copy(
            wo_hbm.at[pl.ds(0, half), pl.ds(QCOLS, rest)],
            w.at[pl.ds(2 * half, half), pl.ds(0, rest)],
            wo_sem.at[1],
        ),
        pltpu.make_async_copy(
            wo_hbm.at[pl.ds(half, half), pl.ds(QCOLS, rest)],
            w.at[pl.ds(2 * half, half), pl.ds(rest, rest)],
            wo_sem.at[2],
        ),
    ]
    for load in wo_loads:
        load.start()
    for load in late_loads:
        load.wait()

    queries = acc[...].astype(jnp.bfloat16)
    placed = dot(sq[0], queries[:, 0:DH])
    placed = placed + dot(sq[1], queries[:, DH : 2 * DH])
    placed = placed + dot(sq[2], queries[:, 2 * DH : 3 * DH])
    q_out[...] = placed.astype(jnp.bfloat16).reshape(GROUP, 16, DH)
    q_copy = spread(q_out, q_in, q_send, q_recv)

    collect(kv_out, kv_in, kv_send, kv_recv)
    fresh = kv_in[0]
    for source in range(1, GROUP):
        fresh = fresh + kv_in[source]
    fresh = fresh.astype(jnp.bfloat16).astype(jnp.float32)
    blank = jnp.zeros((120, DH), jnp.float32)
    fresh_keys = jnp.concatenate([fresh, blank], axis=0).astype(jnp.bfloat16)
    fresh_values = jnp.concatenate([fresh[4:8], fresh[0:4], blank], axis=0).astype(jnp.bfloat16)

    collect(q_out, q_in, q_send, q_recv)
    wide = q_in[...].astype(jnp.float32)
    scale = DH ** (-0.5)
    column_at = lax.broadcasted_iota(jnp.int32, (128, CACHE), 1)
    recent_at = lax.broadcasted_iota(jnp.int32, (128, 128), 1)
    place = lax.rem(lax.broadcasted_iota(jnp.int32, (128, 128), 0), 8)
    step_at = jnp.where(place >= 3, 1, 0)
    results = []
    for r in range(2):
        q = wide[:, r * 8 : r * 8 + 8, :].reshape(128, DH).astype(jnp.bfloat16)
        cached = jnp.where(column_at < len_ref[r], dot_t(q, kc[r]) * scale, -jnp.inf)
        seen = jnp.logical_and(recent_at >= 2 * r, recent_at - 2 * r <= step_at)
        recent = jnp.where(seen, dot_t(q, fresh_keys) * scale, -jnp.inf)
        top = jnp.maximum(jnp.max(cached, -1, keepdims=True), jnp.max(recent, -1, keepdims=True))
        cached_exp = jnp.exp(cached - top)
        recent_exp = jnp.exp(recent - top)
        denom = jnp.sum(cached_exp, -1, keepdims=True) + jnp.sum(recent_exp, -1, keepdims=True)
        inverse = 1.0 / denom
        result = dot((cached_exp * inverse).astype(jnp.bfloat16), vc[r])
        result = result + dot((recent_exp * inverse).astype(jnp.bfloat16), fresh_values)
        results.append(result.astype(jnp.bfloat16))
    ag[me] = dot(pack[...], jnp.concatenate(results, axis=0)).astype(jnp.bfloat16)

    gathered = Gather(ag, a_send, a_recv)
    gathered.step_line(0)
    gathered.step_line(1)
    gathered.step_across(0)
    gathered.step_line(2)
    gathered.step_across(1)
    gathered.step_line(3)
    gathered.step_across(2)
    gathered.step_across(3)
    for k in range(4):
        gathered.sibling(k, 0)
        gathered.sibling(k, 1)
    for load in wo_loads:
        load.wait()

    oacc[...] = jnp.zeros_like(oacc)
    for upper in range(2):

        def heads(i, carry):
            g = i + upper * 6
            block = ag[:, pl.ds(pl.multiple_of(g * 16, 16), 16), :].reshape(256, DH)
            block = dot(unpack[...], block).astype(jnp.bfloat16)
            left = oacc[:, 0:QCOLS]
            right = oacc[:, QCOLS:WIDTH]
            for h in range(4):
                lhs = block[h * 64 : h * 64 + 64]
                rows = pl.ds(pl.multiple_of((g * 4 + h) * DH, DH), DH)
                left = left + dot(lhs, w[rows, :])
                rows = pl.ds(pl.multiple_of(2 * half + (i * 4 + h) * DH, DH), DH)
                right = right + dot(lhs, w[rows, upper * rest : upper * rest + rest])
            oacc[:, 0:QCOLS] = left
            oacc[:, QCOLS:WIDTH] = right
            return carry

        lax.fori_loop(0, 6, heads, 0)
    o_ref[...] = oacc[...].astype(jnp.bfloat16)

    for step in range(1, GROUP):
        st_copy(step).wait_send()
        kv_copy(step).wait_send()
        q_copy(step).wait_send()
    xs.drain()
    gathered.drain()


def fused(inputs, gain, w_query, w_keyval, w_out, key_cache, value_cache, lengths):
    anywhere = pl.BlockSpec(memory_space=pl.ANY)
    vmem = pl.BlockSpec(memory_space=pltpu.VMEM)
    smem = pl.BlockSpec(memory_space=pltpu.SMEM)
    bf16, f32 = jnp.bfloat16, jnp.float32
    dma = pltpu.SemaphoreType.DMA
    out = pl.pallas_call(
        fused_kernel,
        out_shape=jax.ShapeDtypeStruct((PART_ROWS, WIDTH), bf16),
        in_specs=[anywhere, vmem] + [anywhere] * 5 + [smem] + [anywhere] * 4,
        out_specs=vmem,
        scratch_shapes=[
            pltpu.VMEM((GROUP, PART_ROWS, WIDTH), bf16),
            pltpu.VMEM((D, QCOLS), bf16),
            pltpu.VMEM((WIDTH, 2 * DH), bf16),
            pltpu.VMEM((2, CACHE, DH), bf16),
            pltpu.VMEM((2, CACHE, DH), bf16),
            pltpu.VMEM((3, 256, 64), bf16),
            pltpu.VMEM((128, 64), bf16),
            pltpu.VMEM((192, 256), bf16),
            pltpu.VMEM((256, 256), bf16),
            pltpu.VMEM((16, 128), f32),
            pltpu.VMEM((GROUP, 16, 128), f32),
            pltpu.VMEM((GROUP, 8, DH), f32),
            pltpu.VMEM((GROUP, 8, DH), f32),
            pltpu.VMEM((GROUP, 16, DH), bf16),
            pltpu.VMEM((GROUP, 16, DH), bf16),
            pltpu.VMEM((GROUP, 192, DH), bf16),
            pltpu.VMEM((PART_ROWS, 2 * WIDTH), bf16),
            pltpu.VMEM((PART_ROWS, QCOLS), f32),
            pltpu.VMEM((PART_ROWS, WIDTH), f32),
            dma((8,)),
            dma((8,)),
            dma((3,)),
            dma((4, 5)),
            dma((GROUP,)),
            dma((4, 5)),
            dma((GROUP,)),
            dma((GROUP,)),
            dma((GROUP,)),
            dma((GROUP,)),
            dma((GROUP,)),
            dma((GROUP,)),
            dma((GROUP,)),
        ],
        compiler_params=pltpu.CompilerParams(
            collective_id=0, has_side_effects=True, vmem_limit_bytes=56 * 1024 * 1024
        ),
    )(
        inputs.reshape(PART_ROWS, WIDTH),
        gain.astype(f32).reshape(9, 128),
        w_query,
        w_keyval,
        w_out,
        key_cache,
        value_cache,
        lengths,
        *one_hots(),
    )
    return out.reshape(inputs.shape)


def either(inputs, gain, w_query, w_keyval, w_out, key_cache, value_cache, lengths):
    fits = (
        inputs.shape == (2, 32, WIDTH)
        and w_query.shape == (D, QCOLS)
        and w_out.shape == (H * DH, WIDTH)
        and key_cache.shape == (2, CACHE, DH)
    )
    chosen = fused if fits else body
    return chosen(inputs, gain, w_query, w_keyval, w_out, key_cache, value_cache, lengths)


def solution(mesh):
    in_specs = (
        P(None, "rep", "gx"),
        P("gx"),
        P(None, "gx"),
        P("gx", None),
        P(None, "gx"),
        P(("rep", "gx"), None, None),
        P(("rep", "gx"), None, None),
        P(("rep", "gx")),
    )
    out_specs = P(None, "rep", "gx")
    return jax.shard_map(either, mesh=mesh, in_specs=in_specs, out_specs=out_specs, check_vma=False)
```

```python
import jax
import jax.numpy as jnp
import numpy as np
from jax import lax
from jax.experimental import pallas as pl
from jax.experimental.pallas import tpu as pltpu
from jax.sharding import PartitionSpec as P

D = 18432
H = 48
DH = 256
CACHE = 2048


EPS = 1e-05


def collect_keyval(local_normed, w_keyval):
    summed = lax.psum_scatter(
        jnp.einsum("srk,kc->rsc", local_normed, w_keyval, preferred_element_type=jnp.float32),
        "gx",
        scatter_dimension=0,
        tiled=True,
    )
    return jnp.transpose(summed, (1, 0, 2)).astype(jnp.bfloat16)


def project(block, gain, w_query, w_keyval):
    widened = block.astype(jnp.float32)
    totals, squares = lax.psum((jnp.sum(widened, -1), jnp.sum(widened * widened, -1)), "gx")
    row_mean = (totals / D)[..., None]
    row_square = (squares / D)[..., None]
    normed = (
        (widened - row_mean)
        * lax.rsqrt(row_square - row_mean * row_mean + EPS)
        * gain.astype(jnp.float32)
    ).astype(jnp.bfloat16)
    portion = lax.all_gather(normed, "gx", axis=2, tiled=True)
    flat = portion.reshape(-1, portion.shape[2])
    query_part = jnp.dot(flat, w_query, preferred_element_type=jnp.float32).reshape(
        block.shape[0], block.shape[1], w_query.shape[1]
    )
    keyvals = collect_keyval(normed, w_keyval)
    return (query_part.astype(jnp.bfloat16), keyvals)


def attend(queries, key_cache, value_cache, lengths, fresh_keys, fresh_values):
    steps = queries.shape[0]
    rows_here = queries.shape[1]
    scale = DH ** (-0.5)
    grid = queries.reshape(steps, rows_here, H, DH)
    cached = (
        jnp.einsum("srhd,rcd->srhc", grid, key_cache, preferred_element_type=jnp.float32) * scale
    )
    valid = (
        lax.broadcasted_iota(jnp.int32, (1, rows_here, 1, key_cache.shape[1]), 3)
        < lengths[None, :, None, None]
    )
    cached = jnp.where(valid, cached, -jnp.inf)
    recent = (
        jnp.einsum("srhd,trd->srht", grid, fresh_keys, preferred_element_type=jnp.float32) * scale
    )
    allowed = lax.broadcasted_iota(jnp.int32, (steps, 1, 1, steps), 3) <= lax.broadcasted_iota(
        jnp.int32, (steps, 1, 1, steps), 0
    )
    recent = jnp.where(allowed, recent, -jnp.inf)
    top = jnp.maximum(jnp.max(cached, -1, keepdims=True), jnp.max(recent, -1, keepdims=True))
    cached_exp = jnp.exp(cached - top)
    recent_exp = jnp.exp(recent - top)
    denom = jnp.sum(cached_exp, -1, keepdims=True) + jnp.sum(recent_exp, -1, keepdims=True)
    cached_prob = (cached_exp / denom).astype(jnp.bfloat16)
    recent_prob = (recent_exp / denom).astype(jnp.bfloat16)
    result = jnp.einsum(
        "srhc,rcd->srhd", cached_prob, value_cache, preferred_element_type=jnp.float32
    )
    result = result + jnp.einsum(
        "srht,trd->srhd", recent_prob, fresh_values, preferred_element_type=jnp.float32
    )
    return result.astype(jnp.bfloat16).reshape(steps, rows_here, H * DH)


def finish(attended, w_out):
    portion = lax.all_gather(attended, "gx", axis=1, tiled=True)
    flat = portion.reshape(-1, portion.shape[2])
    product = jnp.dot(flat, w_out, preferred_element_type=jnp.float32)
    return product.reshape(portion.shape[0], portion.shape[1], w_out.shape[1]).astype(jnp.bfloat16)


def body(inputs, gain, w_query, w_keyval, w_out, key_cache, value_cache, lengths):
    queries, keyvals = project(inputs, gain, w_query, w_keyval)
    queries = lax.all_to_all(queries, "gx", split_axis=1, concat_axis=2, tiled=True)
    attended = attend(
        queries, key_cache, value_cache, lengths, keyvals[:, :, :DH], keyvals[:, :, DH:]
    )
    return finish(attended, w_out)


GROUP = 16
UNROLL = 6
PIECES = 2
WIDTH = 1152
PART_ROWS = 64
QCOLS = 768
MESH = pl.DeviceIdType.MESH


def one_hots():
    scatter_q = np.zeros((3, 256, 64), np.float32)
    scatter_kv = np.zeros((128, 64), np.float32)
    pack = np.zeros((192, 256), np.float32)
    unpack = np.zeros((256, 256), np.float32)
    for j in range(16):
        for r in range(2):
            for s in range(2):
                row = s * 32 + 2 * j + r
                scatter_kv[j * 8 + r * 2 + s, row] = 1
                scatter_kv[j * 8 + 4 + r * 2 + s, row] = 1
                for h in range(3):
                    scatter_q[h, j * 16 + r * 8 + s * 3 + h, row] = 1
                    pack[(j * 3 + h) * 4 + r * 2 + s, r * 128 + j * 8 + s * 3 + h] = 1
                for h in range(4):
                    unpack[h * 64 + row, j * 16 + h * 4 + r * 2 + s] = 1
    return tuple(jnp.asarray(a, jnp.bfloat16) for a in (scatter_q, scatter_kv, pack, unpack))


def dot(a, b):
    return jnp.dot(a, b, preferred_element_type=jnp.float32)


def dot_t(a, b):
    return lax.dot_general(a, b, (((1,), (1,)), ((), ())), preferred_element_type=jnp.float32)


def fused_kernel(
    x_hbm, g_ref, wq_hbm, wkv_hbm, wo_hbm, kc_hbm, vc_hbm, len_ref, sq_hbm, skv_hbm, pack_hbm, unpack_hbm,
    o_ref,
    xg, w, wkv, kc, vc, sq, skv, pack, unpack, st_out, st_in, kv_out, kv_in, q_out, q_in, ag, lhs_of, xn, acc, oacc,
    load_sem, wq_sem, wo_sem, x_send, x_recv, a_send, a_recv, st_send, st_recv, kv_send, kv_recv, q_send, q_recv,
):
    me = lax.axis_index("gx")
    z = lax.div(me, 4)
    y = lax.rem(lax.div(me, 2), 2)
    c = lax.rem(me, 2)

    def slot_of(zo, yo, co):
        return zo * 4 + yo * 2 + co

    def order(k):
        near = jnp.minimum(z, 3 - z)
        o = k if k >= 2 else jnp.where(near == 0, k, 1 - k)
        return jnp.where(z >= 2, 3 - o, o)

    own_load = pltpu.make_async_copy(x_hbm, xg.at[me], load_sem.at[0])
    own_load.start()
    wkv_load = pltpu.make_async_copy(wkv_hbm, wkv, load_sem.at[1])
    wkv_load.start()
    skv_load = pltpu.make_async_copy(skv_hbm, skv, load_sem.at[2])
    skv_load.start()

    def wq_load(chip):
        rows = pl.ds(pl.multiple_of(chip * (2 * WIDTH), 2 * WIDTH), 2 * WIDTH)
        return pltpu.make_async_copy(wq_hbm.at[rows], w.at[rows], wq_sem.at[chip])

    chips = [(0, 0), (0, 1), (1, 0), (1, 1), (2, 0), (2, 1), (3, 0), (3, 1)]

    def chip_of(k, flip):
        return order(k) * 2 + (1 - y if flip else y)

    for k, flip in chips:
        wq_load(chip_of(k, flip)).start()
    late_loads = [
        pltpu.make_async_copy(sq_hbm, sq, load_sem.at[3]),
        pltpu.make_async_copy(kc_hbm, kc, load_sem.at[4]),
        pltpu.make_async_copy(vc_hbm, vc, load_sem.at[5]),
        pltpu.make_async_copy(pack_hbm, pack, load_sem.at[6]),
        pltpu.make_async_copy(unpack_hbm, unpack, load_sem.at[7]),
    ]
    for load in late_loads:
        load.start()

    barrier = pltpu.get_barrier_semaphore()
    for step in range(1, GROUP):
        pl.semaphore_signal(
            barrier, inc=1, device_id={"gx": lax.rem(me + step, GROUP)}, device_id_type=MESH
        )
    pl.semaphore_wait(barrier, GROUP - 1)

    def remote(src, dst, send, recv, dev):
        return pltpu.make_async_remote_copy(
            src_ref=src, dst_ref=dst, send_sem=send, recv_sem=recv, device_id={"gx": dev}, device_id_type=MESH
        )

    class Gather:
        def __init__(self, buf, send, recv, pieces):
            self.buf, self.send, self.recv, self.pieces = buf, send, recv, pieces
            self.rows = buf.shape[1] // pieces

        def copy(self, slot, k, p, kind, dev):
            block = self.buf.at[slot, pl.ds(p * self.rows, self.rows)]
            return remote(block, block, self.send.at[k, p, kind], self.recv.at[slot, p], dev)

        def arrive(self, slot, p):
            self.copy(slot, 0, p, 0, lax.rem(me + 1, GROUP)).wait_recv()

        def own_across(self):
            return self.copy(me, 0, 0, 2, slot_of(z, 1 - y, c))

        def line(self, k, p, act, skip=False):
            zo = order(k)
            slot = slot_of(zo, y, c)

            @pl.when(jnp.logical_and(zo <= z, z < 3))
            def _():
                act(self.copy(slot, k, p, 0, slot_of(z + 1, y, c)))

            @pl.when(jnp.logical_and(zo >= z, z > 0))
            def _():
                act(self.copy(slot, k, p, 1, slot_of(z - 1, y, c)))

            if not skip:
                act(self.copy(slot, k, p, 2, slot_of(z, 1 - y, c)))
            act(self.copy(slot, k, p, 3, slot_of(z, y, 1 - c)))

        def across(self, k, p, act):
            act(self.copy(slot_of(order(k), 1 - y, c), k, p, 4, slot_of(z, y, 1 - c)))

        def step(self, k):
            for p in range(self.pieces):
                if k < 4:
                    if k > 0:
                        self.arrive(slot_of(order(k), y, c), p)
                    self.line(k, p, lambda copy: copy.start())
                if k == 0 and p == 0:
                    self.own_across().wait_send()
                if k > 0:
                    self.arrive(slot_of(order(k - 1), 1 - y, c), p)
                    self.across(k - 1, p, lambda copy: copy.start())

        def sibling(self, k, flip, pieces=range(PIECES)):
            for p in pieces:
                self.arrive(slot_of(order(k), 1 - y if flip else y, 1 - c), p)

        def drain(self):
            for k in range(4):
                for p in range(self.pieces):
                    self.line(k, p, lambda copy: copy.wait_send(), k == 0 and p == 0)
                    self.across(k, p, lambda copy: copy.wait_send())

    def spread(out, into, send, recv):
        def copy(step):
            target = lax.rem(me + step, GROUP)
            return remote(out.at[target], into.at[me], send.at[step], recv.at[me], target)

        for step in range(1, GROUP):
            copy(step).start()
        into[me] = out[me]
        return copy

    def collect(out, into, send, recv):
        for step in range(1, GROUP):
            source = lax.rem(me + step, GROUP)
            remote(out.at[source], into.at[source], send.at[step], recv.at[source], source).wait_recv()

    xs = Gather(xg, x_send, x_recv, PIECES)
    own_load.wait()
    xs.step(0)

    x = xg[me]
    eye = lax.broadcasted_iota(jnp.int32, (PART_ROWS, PART_ROWS), 0) == lax.broadcasted_iota(
        jnp.int32, (PART_ROWS, PART_ROWS), 1
    )
    squares = jnp.sum(jnp.where(eye, dot_t(x, x), 0.0), axis=0, keepdims=True)
    sums = dot_t(jnp.ones((8, WIDTH), jnp.bfloat16), x)
    st_out[...] = jnp.zeros_like(st_out)
    st_out[0:9, :] = g_ref[...].astype(jnp.float32).reshape(9, 128)
    st_out[9:10, 0:PART_ROWS] = sums[0:1]
    st_out[10:11, 0:PART_ROWS] = squares

    def st_copy(step):
        target = lax.rem(me + step, GROUP)
        return remote(st_out, st_in.at[me], st_send.at[step], st_recv.at[me], target)

    for step in range(1, GROUP):
        st_copy(step).start()
    st_in[me] = st_out[...]
    xs.step(1)
    for step in range(1, GROUP):
        source = lax.rem(me + step, GROUP)
        remote(st_out, st_in.at[source], st_send.at[step], st_recv.at[source], source).wait_recv()

    total = st_in[0]
    for source in range(1, GROUP):
        total = total + st_in[source]

    def column(row):
        spread_row = jnp.broadcast_to(row, (PART_ROWS, PART_ROWS))
        return jnp.sum(jnp.where(eye, spread_row, 0.0), axis=1, keepdims=True)

    mean = column(total[9:10, 0:PART_ROWS]) / D
    square = column(total[10:11, 0:PART_ROWS]) / D
    factor = lax.rsqrt(square - mean * mean + EPS)

    def normed(slot):
        parts = st_in[slot]
        gain = jnp.concatenate([parts[i : i + 1, :] for i in range(9)], axis=1)
        return ((xg[slot].astype(jnp.float32) - mean) * factor * gain).astype(jnp.bfloat16)

    wkv_load.wait()
    skv_load.wait()
    ordered = dot(skv[...], normed(me)).astype(jnp.bfloat16)
    partial = dot(ordered, wkv[...])
    is_key = lax.rem(lax.broadcasted_iota(jnp.int32, (128, DH), 0), 8) < 4
    kv_out[...] = jnp.where(is_key, partial[:, :DH], partial[:, DH:]).reshape(GROUP, 8, DH)
    kv_copy = spread(kv_out, kv_in, kv_send, kv_recv)

    acc[...] = jnp.zeros_like(acc)

    def multiply(k, flip):
        chip = chip_of(k, flip)
        xs.sibling(k, flip)
        xn[:, 0:WIDTH] = normed(chip * 2)
        xn[:, WIDTH : 2 * WIDTH] = normed(chip * 2 + 1)
        wq_load(chip).wait()

        rows = pl.ds(pl.multiple_of(chip * (2 * WIDTH), 2 * WIDTH), 2 * WIDTH)
        acc[...] += dot(xn[...], w[rows, :])

    xs.step(2)
    multiply(0, 0)
    multiply(0, 1)
    multiply(1, 0)
    xs.step(3)
    multiply(1, 1)
    multiply(2, 0)
    multiply(2, 1)
    multiply(3, 0)
    xs.step(4)
    multiply(3, 1)

    half = H * DH // 2
    rest = WIDTH - QCOLS
    wo_loads = [
        pltpu.make_async_copy(wo_hbm.at[:, pl.ds(0, QCOLS)], w.at[pl.ds(0, 2 * half)], wo_sem.at[0]),
        pltpu.make_async_copy(
            wo_hbm.at[pl.ds(0, half), pl.ds(QCOLS, rest)],
            w.at[pl.ds(2 * half, half), pl.ds(0, rest)],
            wo_sem.at[1],
        ),
        pltpu.make_async_copy(
            wo_hbm.at[pl.ds(half, half), pl.ds(QCOLS, rest)],
            w.at[pl.ds(2 * half, half), pl.ds(rest, rest)],
            wo_sem.at[2],
        ),
    ]
    for load in wo_loads:
        load.start()
    for load in late_loads:
        load.wait()

    queries = acc[...].astype(jnp.bfloat16)
    placed = dot(sq[0], queries[:, 0:DH])
    placed = placed + dot(sq[1], queries[:, DH : 2 * DH])
    placed = placed + dot(sq[2], queries[:, 2 * DH : 3 * DH])
    q_out[...] = placed.astype(jnp.bfloat16).reshape(GROUP, 16, DH)
    q_copy = spread(q_out, q_in, q_send, q_recv)

    collect(kv_out, kv_in, kv_send, kv_recv)
    fresh = kv_in[0]
    for source in range(1, GROUP):
        fresh = fresh + kv_in[source]
    fresh = fresh.astype(jnp.bfloat16).astype(jnp.float32)
    blank = jnp.zeros((120, DH), jnp.float32)
    fresh_keys = jnp.concatenate([fresh, blank], axis=0).astype(jnp.bfloat16)
    fresh_values = jnp.concatenate([fresh[4:8], fresh[0:4], blank], axis=0).astype(jnp.bfloat16)

    collect(q_out, q_in, q_send, q_recv)
    wide = q_in[...].astype(jnp.float32)
    scale = DH ** (-0.5)
    column_at = lax.broadcasted_iota(jnp.int32, (128, CACHE), 1)
    recent_at = lax.broadcasted_iota(jnp.int32, (128, 128), 1)
    place = lax.rem(lax.broadcasted_iota(jnp.int32, (128, 128), 0), 8)
    step_at = jnp.where(place >= 3, 1, 0)
    results = []
    for r in range(2):
        q = wide[:, r * 8 : r * 8 + 8, :].reshape(128, DH).astype(jnp.bfloat16)
        cached = jnp.where(column_at < len_ref[r], dot_t(q, kc[r]) * scale, -jnp.inf)
        seen = jnp.logical_and(recent_at >= 2 * r, recent_at - 2 * r <= step_at)
        recent = jnp.where(seen, dot_t(q, fresh_keys) * scale, -jnp.inf)
        top = jnp.maximum(jnp.max(cached, -1, keepdims=True), jnp.max(recent, -1, keepdims=True))
        cached_exp = jnp.exp(cached - top)
        recent_exp = jnp.exp(recent - top)
        denom = jnp.sum(cached_exp, -1, keepdims=True) + jnp.sum(recent_exp, -1, keepdims=True)
        inverse = 1.0 / denom
        result = dot((cached_exp * inverse).astype(jnp.bfloat16), vc[r])
        result = result + dot((recent_exp * inverse).astype(jnp.bfloat16), fresh_values)
        results.append(result.astype(jnp.bfloat16))
    ag[me] = dot(pack[...], jnp.concatenate(results, axis=0)).astype(jnp.bfloat16)

    gathered = Gather(ag, a_send, a_recv, PIECES)
    for k in range(5):
        gathered.step(k)
    for load in wo_loads:
        load.wait()

    oacc[...] = jnp.zeros_like(oacc)
    for upper in range(PIECES):
        for k in range(4):
            gathered.sibling(k, 0, (upper,))
            gathered.sibling(k, 1, (upper,))

        def heads(i, carry):
            for n in range(UNROLL):
                t = i * UNROLL + n
                g = t + upper * 6
                block = ag[:, pl.ds(pl.multiple_of(g * 16, 16), 16), :].reshape(256, DH)
                lhs_of[n] = dot(unpack[...], block).astype(jnp.bfloat16)
            left = oacc[:, 0:QCOLS]
            right = oacc[:, QCOLS:WIDTH]
            for n in range(UNROLL):
                t = i * UNROLL + n
                g = t + upper * 6
                for h in range(4):
                    lhs = lhs_of[n, h * 64 : h * 64 + 64]
                    rows = pl.ds(pl.multiple_of((g * 4 + h) * DH, DH), DH)
                    left = left + dot(lhs, w[rows, :])
                    rows = pl.ds(pl.multiple_of(2 * half + (t * 4 + h) * DH, DH), DH)
                    right = right + dot(lhs, w[rows, upper * rest : upper * rest + rest])
            oacc[:, 0:QCOLS] = left
            oacc[:, QCOLS:WIDTH] = right
            return carry

        lax.fori_loop(0, 6 // UNROLL, heads, 0)
    o_ref[...] = oacc[...].astype(jnp.bfloat16)

    for step in range(1, GROUP):
        st_copy(step).wait_send()
        kv_copy(step).wait_send()
        q_copy(step).wait_send()
    xs.drain()
    gathered.drain()


def fused(inputs, gain, w_query, w_keyval, w_out, key_cache, value_cache, lengths):
    anywhere = pl.BlockSpec(memory_space=pl.ANY)
    vmem = pl.BlockSpec(memory_space=pltpu.VMEM)
    smem = pl.BlockSpec(memory_space=pltpu.SMEM)
    bf16, f32 = jnp.bfloat16, jnp.float32
    dma = pltpu.SemaphoreType.DMA
    out = pl.pallas_call(
        fused_kernel,
        out_shape=jax.ShapeDtypeStruct((PART_ROWS, WIDTH), bf16),
        in_specs=[anywhere, vmem] + [anywhere] * 5 + [smem] + [anywhere] * 4,
        out_specs=vmem,
        scratch_shapes=[
            pltpu.VMEM((GROUP, PART_ROWS, WIDTH), bf16),
            pltpu.VMEM((D, QCOLS), bf16),
            pltpu.VMEM((WIDTH, 2 * DH), bf16),
            pltpu.VMEM((2, CACHE, DH), bf16),
            pltpu.VMEM((2, CACHE, DH), bf16),
            pltpu.VMEM((3, 256, 64), bf16),
            pltpu.VMEM((128, 64), bf16),
            pltpu.VMEM((192, 256), bf16),
            pltpu.VMEM((256, 256), bf16),
            pltpu.VMEM((16, 128), f32),
            pltpu.VMEM((GROUP, 16, 128), f32),
            pltpu.VMEM((GROUP, 8, DH), f32),
            pltpu.VMEM((GROUP, 8, DH), f32),
            pltpu.VMEM((GROUP, 16, DH), bf16),
            pltpu.VMEM((GROUP, 16, DH), bf16),
            pltpu.VMEM((GROUP, 192, DH), bf16),
            pltpu.VMEM((UNROLL, 256, DH), bf16),
            pltpu.VMEM((PART_ROWS, 2 * WIDTH), bf16),
            pltpu.VMEM((PART_ROWS, QCOLS), f32),
            pltpu.VMEM((PART_ROWS, WIDTH), f32),
            dma((8,)),
            dma((8,)),
            dma((3,)),
            dma((4, PIECES, 5)),
            dma((GROUP, PIECES)),
            dma((4, PIECES, 5)),
            dma((GROUP, PIECES)),
            dma((GROUP,)),
            dma((GROUP,)),
            dma((GROUP,)),
            dma((GROUP,)),
            dma((GROUP,)),
            dma((GROUP,)),
        ],
        compiler_params=pltpu.CompilerParams(
            collective_id=0, has_side_effects=True, vmem_limit_bytes=56 * 1024 * 1024
        ),
    )(
        inputs.reshape(PART_ROWS, WIDTH),
        gain,
        w_query,
        w_keyval,
        w_out,
        key_cache,
        value_cache,
        lengths,
        *one_hots(),
    )
    return out.reshape(inputs.shape)


def either(inputs, gain, w_query, w_keyval, w_out, key_cache, value_cache, lengths):
    fits = (
        inputs.shape == (2, 32, WIDTH)
        and w_query.shape == (D, QCOLS)
        and w_out.shape == (H * DH, WIDTH)
        and key_cache.shape == (2, CACHE, DH)
    )
    chosen = fused if fits else body
    return chosen(inputs, gain, w_query, w_keyval, w_out, key_cache, value_cache, lengths)


def solution(mesh):
    in_specs = (
        P(None, "rep", "gx"),
        P("gx"),
        P(None, "gx"),
        P("gx", None),
        P(None, "gx"),
        P(("rep", "gx"), None, None),
        P(("rep", "gx"), None, None),
        P(("rep", "gx")),
    )
    out_specs = P(None, "rep", "gx")
    return jax.shard_map(either, mesh=mesh, in_specs=in_specs, out_specs=out_specs, check_vma=False)
```
